128 devices in a mesh: gx: 8 (over x, core), gy: 16 (over y, z).
Axes of the slice: x: 4, y: 4, z: 4, core: 2. Of those that a mesh axis runs over, the one named last changes fastest.
Arguments:
- charges: bfloat16 [128, 8192, 128], P(('gx', 'gy')), may hold values from -6 to 6
- leaf_slot: int32 [128, 8192], P(('gx', 'gy')), may hold values from 0 to 8191, each once within a row
- node_offset: bfloat16 [128, 2, 8192], P(('gx', 'gy')), may hold values from -3.140625 to 3.140625
- lagrange: bfloat16 [2, 2, 2, 64, 64], replicated, may hold values from -0.375 to 0.375
- evaluate: bfloat16 [2, 64, 64], replicated, may hold values from -0.5 to 0.5
Outputs:
- target_field: bfloat16 [8192, 128, 128], P(('gx', 'gy'))
The draws below stay inside these ranges and needn't reach their ends.
Inputs may be any that keep to these rules, and one draw needn't show every extreme that they name: Each block's row leaf_slot[b] is a permutation of 0 to 8191.
All inputs are finite; a program needn't handle non-finite values.
Results may differ from the reference program's by a relative error of at most 0.035.
Values may be sent and summed in bfloat16 or wider, within the bound.
A program may use at most 128 MiB of HBM per device.

```python
import math
import jax
import jax.numpy as jnp
from jax import lax

P_SIZE = 64
M = 64
NODES = 8192
BLOCKS = 128


def block_levels(own_key, dims, shards, low, largest):
    def one(axis_at, parts):
        draws = jax.random.uniform(jax.random.fold_in(jax.random.fold_in(own_key, 6), axis_at), (parts,), jnp.float32, low / len(shards), largest / len(shards))
        return jnp.repeat(jnp.exp(draws), dims[axis_at] // parts).reshape((-1,) + (1,) * (len(dims) - axis_at - 1))

    factor_of = one(*shards[0])
    for cut in shards[1:]:
        factor_of = factor_of * one(*cut)
    return factor_of


def normal_values(key, extent, scale, reach, shards=(), kind=jnp.bfloat16):
    result = jax.random.normal(key, extent, jnp.float32) * scale
    if len(shards) > 0:
        result = block_levels(key, extent, shards, -0.22, 0.18) * result
    return jnp.clip(result, min=-reach, max=reach).astype(kind)


def setup_inputs(seed: int = 0) -> dict:
    key_of = jax.random.split(jax.random.key(seed), 6)
    return {
        "charges": normal_values(key_of[0], (BLOCKS, NODES, 2 * P_SIZE), 1.0, 6.0, ((0, 128),)),
        "leaf_slot": jax.vmap(lambda own: jax.random.permutation(own, NODES))(jax.random.split(key_of[1], BLOCKS)).reshape((BLOCKS, NODES)).astype(jnp.int32),
        "node_offset": jnp.clip(jax.random.uniform(key_of[2], (BLOCKS, 2, NODES), jnp.float32, -3.140625, 3.140625), -3.140625, 3.140625).astype(jnp.bfloat16),
        "lagrange": normal_values(key_of[3], (2, 2, 2, P_SIZE, P_SIZE), (4 * P_SIZE) ** -0.5, 0.375),
        "evaluate": normal_values(key_of[4], (2, P_SIZE, M), (2 * P_SIZE) ** -0.5, 0.5),
    }


def real_form(complex_parts):
    real_part = complex_parts[..., 0, :, :]
    imag_part = complex_parts[..., 1, :, :]
    upper = jnp.concatenate([real_part, imag_part], axis=-1)
    lower = jnp.concatenate([-imag_part, real_part], axis=-1)
    return jnp.concatenate([upper, lower], axis=-2)

def turn(current, offsets, factor):
    half_width = current.shape[-1] // 2
    side_count = math.isqrt(half_width)
    positions = jnp.arange(side_count, dtype=jnp.float32)
    chebyshev = jnp.cos(math.pi * (2.0 * positions + 1.0) / (2.0 * side_count))
    row_nodes = jnp.repeat(chebyshev, side_count)
    col_nodes = jnp.tile(chebyshev, side_count)
    first_term = offsets[..., 0, :, None].astype(jnp.float32) * row_nodes
    second = offsets[..., 1, :, None].astype(jnp.float32) * col_nodes
    angles = (first_term + second) * factor
    cosine = jnp.cos(angles)
    sine_part = jnp.sin(angles)
    real_part = current[..., :half_width]
    imag_part = current[..., half_width:]
    return jnp.concatenate([cosine * real_part - sine_part * imag_part, sine_part * real_part + cosine * imag_part], axis=-1).astype(jnp.bfloat16)

def reference(charges, leaf_slot, node_offset, lagrange, evaluate):
    block_count, row_count, width = charges.shape
    ordered = jnp.take_along_axis(charges, leaf_slot[:, :, None], axis=1)
    node_total = block_count * row_count
    current = ordered.reshape(node_total, width).astype(jnp.float32)
    offsets = jnp.transpose(node_offset, (1, 0, 2)).reshape(2, node_total)
    mixing = real_form(lagrange).astype(jnp.float32)
    level_count = node_total.bit_length() - 1
    for level_index in range(level_count):
        phased = turn(current, offsets, level_index + 1).astype(jnp.float32)
        grouped = phased.reshape(node_total >> level_index + 1, 2, 1 << level_index, width)
        current = jnp.einsum('aejf,ecfk->acjk', grouped, mixing, precision=lax.Precision.HIGHEST).reshape(node_total, width)
    finished = turn(current, offsets, level_count + 1)
    values = jnp.dot(finished, real_form(evaluate), preferred_element_type=jnp.float32).astype(jnp.bfloat16)
    return jnp.transpose(values.reshape(block_count, row_count, values.shape[-1]), (1, 0, 2))
```

```python
import functools
import math

import jax
import jax.numpy as jnp
import numpy as np
from jax import lax
from jax.experimental import pallas as pl
from jax.experimental.pallas import tpu as pltpu
from jax.sharding import PartitionSpec as P

MESH = pl.DeviceIdType.MESH
F32 = jnp.float32
BF16 = jnp.bfloat16
TURN = 2.0 * math.pi
SIN_TERMS = None


def sine_terms():
    k = np.arange(400)
    w = 0.125 * (1 + np.cos(np.pi * (k + 0.5) / 400))
    v = w * w
    basis = np.stack([w * v**j for j in range(5)], axis=1)
    weight = 1.0 / np.sqrt(np.sin(TURN * w) + 1e-3)
    coef = np.linalg.lstsq(basis * weight[:, None], np.sin(TURN * w) * weight, rcond=None)[0]
    return [float(c) for c in coef]


SIN_TERMS = sine_terms()
TILES = 8
ROLL16 = True
PARTS = ("gather", "z1", "p1", "z2", "p2", "comm", "z3", "p3")


def cosine_turns(x):
    x = x - jnp.round(x)
    w = 0.25 - jnp.abs(x)
    v = w * w
    r = SIN_TERMS[4] * v + SIN_TERMS[3]
    r = r * v + SIN_TERMS[2]
    r = r * v + SIN_TERMS[1]
    r = r * v + SIN_TERMS[0]
    return r * w


def swap(tile):
    if ROLL16:
        return pltpu.roll(tile, 64, 1)
    return pltpu.roll(tile.astype(F32), 64, 1).astype(BF16)


def kernel(parts, ch_ref, slot_ref, off_ref, lag_ref, ev_ref, nodes_ref, out_ref,
           cf, g, zt, x, send, recv, ab, ro, at, w, ev, ob, o32, ssem, rsem, offs, offr, osem):
    gx, gy = lax.axis_index("gx"), lax.axis_index("gy")
    me = gx * 16 + gy
    comm = "comm" in parts
    if comm:
        bar = pltpu.get_barrier_semaphore()

        @pl.loop(1, 128)
        def _(k):
            dst = (me + k) & 127
            pl.semaphore_signal(bar, inc=1, device_id=(dst >> 4, dst & 15), device_id_type=MESH)

    for e in range(2):
        for c in range(2):
            re = lag_ref[e, c, 0].astype(F32)
            im = lag_ref[e, c, 1].astype(F32)
            w[pl.ds(e * 128, 64), pl.ds(c * 128, 128)] = jnp.concatenate([re, im], axis=1).astype(BF16)
            w[pl.ds(e * 128 + 64, 64), pl.ds(c * 128, 128)] = jnp.concatenate([-im, re], axis=1).astype(BF16)
    re = ev_ref[0].astype(F32)
    im = ev_ref[1].astype(F32)
    ev[pl.ds(0, 64), :] = jnp.concatenate([re, im], axis=1).astype(BF16)
    ev[pl.ds(64, 64), :] = jnp.concatenate([-im, re], axis=1).astype(BF16)

    for m in range(64):
        ab[m] = off_ref[0, :, pl.ds(m * 128, 128)].astype(F32)
    for k in range(2):
        rows = ab[:, k, :]
        at[k] = jnp.concatenate([rows, rows], axis=0).T
        at[2 + k, pl.ds(0, 64)] = rows

    lane = lax.broadcasted_iota(jnp.int32, (16, 128), 1)
    low = lane < 64
    ui = nodes_ref[0:1, :]
    uj = nodes_ref[1:2, :]
    quarter = jnp.where(low, 0.0, -0.25).astype(F32)

    def column(ref, k, row, j):
        return jnp.broadcast_to(pltpu.roll(ref[k, pl.ds(row, 16), :], (128 - j) & 127, 1)[:, 0:1], (16, 128))

    def many_phases(total, place, offset_of, first, count):
        @pl.loop(0, total, step=TILES)
        def _(j):
            spots = [place(j + u) for u in range(TILES)]
            state = []
            for u in range(TILES):
                a, b = offset_of(j + u)
                tau = a * ui + b * uj
                if first == 1:
                    now = cosine_turns(tau + quarter)
                    twice = 2.0 * jnp.where(low, now, pltpu.roll(now, 64, 1))
                    before = jnp.where(low, 1.0, 0.0).astype(F32)
                else:
                    twice = 2.0 * cosine_turns(tau)
                    now = cosine_turns(tau * float(first) + quarter)
                    before = cosine_turns(tau * float(first - 1) + quarter)
                state.append((now, before, twice))
            for l in range(count):
                for u in range(TILES):
                    now, before, twice = state[u]
                    i, q = spots[u]
                    zb = now.astype(BF16)
                    rb = swap(zb)
                    zt[i, l, q, :, pl.ds(0, 128)] = jnp.where(low, zb, rb)
                    zt[i, l, q, :, pl.ds(128, 128)] = jnp.where(low, -rb, zb)
                    if l + 1 < count:
                        state[u] = (twice * now - before, now, twice)

    def turned(tile, i, l, q):
        return tile * zt[i, l, q, :, pl.ds(0, 128)] + swap(tile) * zt[i, l, q, :, pl.ds(128, 128)]

    def level(i, l, bit, load, save, per=32):
        for blk in range(64 // per):
            rows = []
            idx = []
            for p in range(blk * per, (blk + 1) * per):
                q0 = ((p >> bit) << (bit + 1)) | (p & ((1 << bit) - 1))
                q1 = q0 | (1 << bit)
                idx.append((q0, q1))
                rows.append(jnp.concatenate([turned(load(q0), i, l, q0), turned(load(q1), i, l, q1)], axis=1))
            o = jnp.dot(jnp.concatenate(rows, axis=0), w[...], preferred_element_type=F32)
            for j, (q0, q1) in enumerate(idx):
                save(q0, o[16 * j:16 * j + 16, 0:128])
                save(q1, o[16 * j:16 * j + 16, 128:256])

    def load_x(q):
        return x[q]

    def save_x(q, v):
        x[q] = v.astype(BF16)

    @pl.loop(0, 8)
    def _(j):
        cf[pl.ds(j * 1024, 1024), :] = ch_ref[0, pl.ds(j * 1024, 1024), :].astype(F32)

    @pl.loop(0, 4)
    def _(i):
        @pl.loop(0, 128)
        def _(q):
            if "gather" in parts:
                base = i * 2048 + q
                for s in range(16):
                    slot = slot_ref[0, base + s * 128]
                    g[i, q, pl.ds(s, 1), :] = cf[pl.ds(slot, 1), :]

        if "z1" in parts:
            many_phases(128, lambda j: (i, j), lambda j: (column(at, 2, i * 16, j), column(at, 3, i * 16, j)), 1, 7)

    if "p1" in parts:
        @pl.loop(0, 4)
        def _(i):
            for l in range(7):
                load = load_x if l > 0 else (lambda q: g[i, q].astype(BF16))
                if l < 6:
                    save = save_x
                else:
                    def save(q, v):
                        c, t, hi = (q >> 4) & 3, q & 15, q >> 6
                        cf[pl.ds(((c * 64 + 16 * i) * 2 + hi) * 16 + t, 16, stride=32), :] = v
                level(i, l, l, load, save)

    if comm:
        pl.semaphore_wait(bar, 127)

        @pl.loop(1, 128)
        def _(k):
            dst = (me + k) & 127
            pltpu.make_async_remote_copy(src_ref=ab.at[dst >> 1], dst_ref=ro.at[me], send_sem=offs.at[0],
                                         recv_sem=offr.at[0], device_id=(dst >> 4, dst & 15), device_id_type=MESH).start()
        pltpu.make_async_copy(ab.at[me >> 1], ro.at[me], offr.at[0]).start()

    @pl.loop(0, 4)
    def _(c):
        if "z2" in parts:
            many_phases(128, lambda j: (0, j), lambda j: (
                column(at, 0, (j & 1) * 64 + c * 16, j >> 1), column(at, 1, (j & 1) * 64 + c * 16, j >> 1)), 8, 6)
        if "p2" in parts:
            for l in range(6):
                load = load_x if l > 0 else (lambda q: cf[pl.ds((c * 128 + q) * 16, 16), :].astype(BF16))
                if l < 5:
                    save = save_x
                else:
                    def save(q, v):
                        send[c, q] = v.astype(BF16)
                level(0, l, l + 1, load, save)
        if comm:
            @pl.loop(1, 128)
            def _(k):
                dst = (me + k) & 127
                pltpu.make_async_remote_copy(src_ref=send.at[c, dst], dst_ref=recv.at[c, me], send_sem=ssem.at[c],
                                             recv_sem=rsem.at[c], device_id=(dst >> 4, dst & 15), device_id_type=MESH).start()
            pltpu.make_async_copy(send.at[c, me], recv.at[c, me], rsem.at[c]).start()

    if comm:
        pltpu.make_async_copy(ro, ro, offr.at[0]).wait()
    for k in range(2):
        at[k] = ro[:, k, :].T
    half = (me & 1) * 64

    if "z3" in parts:
        @pl.loop(0, 4)
        def _(c):
            row = pl.multiple_of(half + c * 16, 16)
            many_phases(128, lambda j: (c, j), lambda j: (column(at, 0, row, j), column(at, 1, row, j)), 14, 8)

    @pl.loop(0, 4)
    def _(c):
        if comm:
            pltpu.make_async_copy(recv.at[c], recv.at[c], rsem.at[c]).wait()
        if "p3" in parts:
            for l in range(7):
                level(c, l, l, load_x if l > 0 else (lambda q: recv[c, q]), save_x)
            for blk in range(4):
                rows = jnp.concatenate([turned(x[q], c, 7, q) for q in range(blk * 32, blk * 32 + 32)], axis=0)
                v = jnp.dot(rows, ev[...], preferred_element_type=F32)
                for j in range(32):
                    o32[pl.ds(blk * 32 + j, 16, stride=128), :] = v[16 * j:16 * j + 16]
            for t in range(16):
                ob[c, t] = o32[pl.ds(t * 128, 128), :].astype(BF16)
        pltpu.make_async_copy(ob.at[c], out_ref.at[pl.ds(c * 16, 16)], osem.at[c]).start()

    for c in range(4):
        pltpu.make_async_copy(ob.at[c], out_ref.at[pl.ds(c * 16, 16)], osem.at[c]).wait()
    if comm:
        pltpu.make_async_copy(ro.at[pl.ds(0, 127)], ro.at[pl.ds(0, 127)], offs.at[0]).wait()
        for c in range(4):
            pltpu.make_async_copy(recv.at[c, pl.ds(0, 127)], recv.at[c, pl.ds(0, 127)], ssem.at[c]).wait()


def chebyshev_lanes():
    side = 8
    u = np.cos(math.pi * (2.0 * np.arange(side) + 1.0) / (2.0 * side))
    row = np.repeat(u, side)
    col = np.tile(u, side)
    table = np.zeros((8, 128))
    table[0] = np.concatenate([row, row]) / TURN
    table[1] = np.concatenate([col, col]) / TURN
    return table.astype(np.float32)


def body(charges, leaf_slot, node_offset, lagrange, evaluate, parts=PARTS):
    vm = pl.BlockSpec(memory_space=pltpu.VMEM)
    comm = "comm" in parts
    cp = dict(collective_id=0) if comm else {}
    return pl.pallas_call(
        functools.partial(kernel, parts),
        out_shape=jax.ShapeDtypeStruct((64, 128, 128), BF16),
        in_specs=[vm, pl.BlockSpec(memory_space=pltpu.SMEM), vm, vm, vm, vm],
        out_specs=pl.BlockSpec(memory_space=pl.ANY),
        scratch_shapes=[
            pltpu.VMEM((8192, 128), F32),
            pltpu.VMEM((4, 128, 16, 128), F32),
            pltpu.VMEM((4, 8, 128, 16, 256), BF16),
            pltpu.VMEM((128, 16, 128), BF16),
            pltpu.VMEM((4, 128, 16, 128), BF16),
            pltpu.VMEM((4, 128, 16, 128), BF16),
            pltpu.VMEM((64, 2, 128), F32),
            pltpu.VMEM((128, 2, 128), F32),
            pltpu.VMEM((4, 128, 128), F32),
            pltpu.VMEM((256, 256), BF16),
            pltpu.VMEM((128, 128), BF16),
            pltpu.VMEM((4, 16, 128, 128), BF16),
            pltpu.VMEM((2048, 128), F32),
            pltpu.SemaphoreType.DMA((4,)), pltpu.SemaphoreType.DMA((4,)),
            pltpu.SemaphoreType.DMA((1,)), pltpu.SemaphoreType.DMA((1,)), pltpu.SemaphoreType.DMA((4,)),
        ],
        compiler_params=pltpu.CompilerParams(has_side_effects=True, vmem_limit_bytes=60 << 20, **cp),
    )(charges, leaf_slot, node_offset, lagrange, evaluate, jnp.asarray(chebyshev_lanes()))


def solution(mesh, parts=PARTS):
    placed = (P(("gx", "gy"), None, None), P(("gx", "gy"), None), P(("gx", "gy"), None, None), P(), P())
    return jax.shard_map(functools.partial(body, parts=parts), mesh=mesh, in_specs=placed,
                         out_specs=P(("gx", "gy"), None, None), check_vma=False)
```

```python
import functools
import math

import jax
import jax.numpy as jnp
import numpy as np
from jax import lax
from jax.experimental import pallas as pl
from jax.experimental.pallas import tpu as pltpu
from jax.sharding import PartitionSpec as P

MESH = pl.DeviceIdType.MESH
F32 = jnp.float32
BF16 = jnp.bfloat16
TURN = 2.0 * math.pi
SIN_TERMS = None


def sine_terms():
    k = np.arange(400)
    w = 0.125 * (1 + np.cos(np.pi * (k + 0.5) / 400))
    v = w * w
    basis = np.stack([w * v**j for j in range(4)], axis=1)
    weight = 1.0 / np.sqrt(np.sin(TURN * w) + 1e-3)
    coef = np.linalg.lstsq(basis * weight[:, None], np.sin(TURN * w) * weight, rcond=None)[0]
    return [float(c) for c in coef]


SIN_TERMS = sine_terms()
TILES = 8
ROLL16 = True
PARTS = ("gather", "z1", "p1", "z2", "p2", "comm", "z3", "p3")


def cosine_turns(x):
    x = x - jnp.round(x)
    w = 0.25 - jnp.abs(x)
    v = w * w
    r = SIN_TERMS[3] * v + SIN_TERMS[2]
    r = r * v + SIN_TERMS[1]
    r = r * v + SIN_TERMS[0]
    return r * w


def swap(tile):
    if ROLL16:
        return pltpu.roll(tile, 64, 1)
    return pltpu.roll(tile.astype(F32), 64, 1).astype(BF16)


def kernel(parts, ch_ref, slot_ref, off_ref, lag_ref, ev_ref, nodes_ref, out_ref,
           cf, g, zt, x, send, recv, ab, ro, at, lh, lt, us, tau, w, ev, ob, o32, ssem, rsem, offs, offr, osem):
    gx, gy = lax.axis_index("gx"), lax.axis_index("gy")
    me = gx * 16 + gy
    comm = "comm" in parts
    if comm:
        bar = pltpu.get_barrier_semaphore()

        @pl.loop(1, 128)
        def _(k):
            dst = (me + k) & 127
            pl.semaphore_signal(bar, inc=1, device_id=(dst >> 4, dst & 15), device_id_type=MESH)

    for e in range(2):
        for c in range(2):
            re = lag_ref[e, c, 0].astype(F32)
            im = lag_ref[e, c, 1].astype(F32)
            w[pl.ds(e * 128, 64), pl.ds(c * 128, 128)] = jnp.concatenate([re, im], axis=1).astype(BF16)
            w[pl.ds(e * 128 + 64, 64), pl.ds(c * 128, 128)] = jnp.concatenate([-im, re], axis=1).astype(BF16)
    re = ev_ref[0].astype(F32)
    im = ev_ref[1].astype(F32)
    ev[pl.ds(0, 64), :] = jnp.concatenate([re, im], axis=1).astype(BF16)
    ev[pl.ds(64, 64), :] = jnp.concatenate([-im, re], axis=1).astype(BF16)

    none = jnp.zeros((8, 128), F32)
    top = jnp.concatenate([nodes_ref[...], none], axis=1)
    bottom = jnp.concatenate([none, nodes_ref[...]], axis=1)
    us[...] = jnp.zeros((8, 128, 256), BF16)
    for p in range(8):
        us[p, pl.ds(16 * p, 16), :] = jnp.concatenate([top, bottom], axis=0).astype(BF16)

    for m in range(64):
        ab[m] = off_ref[0, :, pl.ds(m * 128, 128)].astype(F32)
    lane = lax.broadcasted_iota(jnp.int32, (16, 128), 1)
    low = lane < 64
    signed = jnp.where(low, 0.25, -0.25).astype(F32)
    wide = lax.broadcasted_iota(jnp.int32, (64, 128), 1) < 64

    def make_tau(oa, ob_):
        for k in range(3):
            lh[pl.ds(2 * k, 64, stride=8), :] = oa
            lh[pl.ds(2 * k + 1, 64, stride=8), :] = ob_
        for k in range(6, 8):
            lh[pl.ds(k, 64, stride=8), :] = jnp.zeros((64, 128), F32)
        for n in range(4):
            lt[pl.ds(n * 128, 128), :] = lh[pl.ds(n * 128, 128), :].T.astype(BF16)

        @pl.loop(0, 8, step=2)
        def _(p):
            for e in range(2):
                r = jnp.dot(lt[...], us[p + e], preferred_element_type=F32)
                for n in range(4):
                    row = pl.multiple_of((n * 16 + 2 * (p + e)) * 128, 128)
                    tau[pl.ds(row, 128), :] = r[n * 128:n * 128 + 128, 0:128]
                    tau[pl.ds(row + 128, 128), :] = r[n * 128:n * 128 + 128, 128:256]

    def start(t, first):
        c1 = cosine_turns(t)
        s1 = cosine_turns(t + signed)
        twice = 2.0 * c1
        if first == 1:
            return (c1, s1), (1.0, 0.0), twice
        c2, s2 = twice * c1 - 1.0, twice * s1
        if first == 8:
            k2 = 2.0 * c2
            c4, s4 = k2 * c2 - 1.0, k2 * s2
            k4 = 2.0 * c4
            c8, s8 = k4 * c4 - 1.0, k4 * s4
            return (c8, s8), (c8 * c1 + s8 * s1, s8 * c1 - c8 * s1), twice
        c3, s3 = twice * c2 - c1, twice * s2 - s1
        k3 = 2.0 * c3
        c6, s6 = k3 * c3 - 1.0, k3 * s3
        c7, s7 = c6 * c1 - s6 * s1, s6 * c1 + c6 * s1
        k7 = 2.0 * c7
        c14, s14 = k7 * c7 - 1.0, k7 * s7
        return (c14, s14), (c14 * c1 + s14 * s1, s14 * c1 - c14 * s1), twice

    def phase_tiles(i, slot, first, count, j, tiles):
        state = [start(tau[pl.ds((j + n) * 64 + i * 16, 16), :], first) for n in range(tiles)]
        for l in range(count):
            for n in range(tiles):
                now, before, twice = state[n]
                zt[slot, l, j + n, :, pl.ds(0, 128)] = now[0].astype(BF16)
                zt[slot, l, j + n, :, pl.ds(128, 128)] = now[1].astype(BF16)
                if l + 1 < count:
                    state[n] = ((twice * now[0] - before[0], twice * now[1] - before[1]), now, twice)

    def many_phases(i, slot, first, count):
        @pl.loop(0, 128, step=TILES)
        def _(j):
            phase_tiles(i, slot, first, count, j, TILES)

    def turned(tile, i, l, q):
        return tile * zt[i, l, q, :, pl.ds(0, 128)] + swap(tile) * zt[i, l, q, :, pl.ds(128, 128)]

    def level(i, l, bit, load, save, per=32):
        for blk in range(64 // per):
            rows = []
            idx = []
            for p in range(blk * per, (blk + 1) * per):
                q0 = ((p >> bit) << (bit + 1)) | (p & ((1 << bit) - 1))
                q1 = q0 | (1 << bit)
                idx.append((q0, q1))
                rows.append(jnp.concatenate([turned(load(q0), i, l, q0), turned(load(q1), i, l, q1)], axis=1))
            o = jnp.dot(jnp.concatenate(rows, axis=0), w[...], preferred_element_type=F32)
            for j, (q0, q1) in enumerate(idx):
                save(q0, o[16 * j:16 * j + 16, 0:128])
                save(q1, o[16 * j:16 * j + 16, 128:256])

    def load_x(q):
        return x[q]

    def save_x(q, v):
        x[q] = v.astype(BF16)

    pair = []
    for k in range(2):
        rows = ab[:, k, :]
        at[...] = jnp.concatenate([rows, rows], axis=0).T
        pair.append(jnp.where(wide, at[pl.ds(0, 64, stride=2), :], at[pl.ds(1, 64, stride=2), :]))
    make_tau(*pair)

    @pl.loop(0, 8)
    def _(j):
        cf[pl.ds(j * 1024, 1024), :] = ch_ref[0, pl.ds(j * 1024, 1024), :].astype(F32)

    @pl.loop(0, 4)
    def _(i):
        @pl.loop(0, 128, step=TILES)
        def _(j):
            if "z1" in parts:
                phase_tiles(i, i, 1, 7, j, TILES)
            if "gather" in parts:
                for n in range(TILES):
                    for r in range(16):
                        slot = slot_ref[0, (i * 16 + r) * 128 + j + n]
                        g[i, j + n, pl.ds(r, 1), :] = cf[pl.ds(slot, 1), :]

    if "p1" in parts:
        @pl.loop(0, 4)
        def _(i):
            for l in range(7):
                load = load_x if l > 0 else (lambda q: g[i, q].astype(BF16))
                if l < 6:
                    save = save_x
                else:
                    def save(q, v):
                        c, t, hi = (q >> 4) & 3, q & 15, q >> 6
                        cf[pl.ds((c * 64 + 16 * i) * 33 + hi * 16 + t, 16, stride=33), :] = v
                level(i, l, l, load, save)

    if comm:
        pl.semaphore_wait(bar, 127)

        @pl.loop(1, 128)
        def _(k):
            dst = (me + k) & 127
            pltpu.make_async_remote_copy(src_ref=ab.at[dst >> 1], dst_ref=ro.at[me], send_sem=offs.at[0],
                                         recv_sem=offr.at[0], device_id=(dst >> 4, dst & 15), device_id_type=MESH).start()
        pltpu.make_async_copy(ab.at[me >> 1], ro.at[me], offr.at[0]).start()

    make_tau(ab[:, 0, :], ab[:, 1, :])

    @pl.loop(0, 4)
    def _(c):
        if "z2" in parts:
            many_phases(c, 0, 8, 6)
        if "p2" in parts:
            for l in range(6):
                load = load_x if l > 0 else (lambda q: cf[pl.ds((c * 64 + (q >> 1)) * 33 + (q & 1) * 16, 16), :].astype(BF16))
                if l < 5:
                    save = save_x
                else:
                    def save(q, v):
                        send[c, q] = v.astype(BF16)
                level(0, l, l + 1, load, save)
        if comm:
            @pl.loop(1, 128)
            def _(k):
                dst = (me + k) & 127
                pltpu.make_async_remote_copy(src_ref=send.at[c, dst], dst_ref=recv.at[c, me], send_sem=ssem.at[c],
                                             recv_sem=rsem.at[c], device_id=(dst >> 4, dst & 15), device_id_type=MESH).start()
            pltpu.make_async_copy(send.at[c, me], recv.at[c, me], rsem.at[c]).start()

    if comm:
        pltpu.make_async_copy(ro, ro, offr.at[0]).wait()
    odd = jnp.full((64, 128), me & 1, jnp.int32) == 1
    pair = []
    for k in range(2):
        first, second = ro[pl.ds(0, 64, stride=2), k, :], ro[pl.ds(1, 64, stride=2), k, :]
        even_half = jnp.where(wide, first, pltpu.roll(second, 64, 1))
        odd_half = jnp.where(wide, pltpu.roll(first, 64, 1), second)
        pair.append(jnp.where(odd, odd_half, even_half))
    make_tau(*pair)

    if "z3" in parts:
        @pl.loop(0, 4)
        def _(c):
            many_phases(c, c, 14, 8)

    @pl.loop(0, 4)
    def _(c):
        if comm:
            pltpu.make_async_copy(recv.at[c], recv.at[c], rsem.at[c]).wait()
        if "p3" in parts:
            for l in range(7):
                level(c, l, l, load_x if l > 0 else (lambda q: recv[c, q]), save_x)
            for blk in range(4):
                rows = jnp.concatenate([turned(x[q], c, 7, q) for q in range(blk * 32, blk * 32 + 32)], axis=0)
                v = jnp.dot(rows, ev[...], preferred_element_type=F32)
                for j in range(32):
                    o32[pl.ds(blk * 32 + j, 16, stride=129), :] = v[16 * j:16 * j + 16]
            for t in range(16):
                ob[c, t] = o32[pl.ds(t * 129, 128), :].astype(BF16)
        pltpu.make_async_copy(ob.at[c], out_ref.at[pl.ds(c * 16, 16)], osem.at[c]).start()

    for c in range(4):
        pltpu.make_async_copy(ob.at[c], out_ref.at[pl.ds(c * 16, 16)], osem.at[c]).wait()
    if comm:
        pltpu.make_async_copy(ro.at[pl.ds(0, 127)], ro.at[pl.ds(0, 127)], offs.at[0]).wait()
        for c in range(4):
            pltpu.make_async_copy(recv.at[c, pl.ds(0, 127)], recv.at[c, pl.ds(0, 127)], ssem.at[c]).wait()


def chebyshev_lanes():
    side = 8
    u = np.cos(math.pi * (2.0 * np.arange(side) + 1.0) / (2.0 * side))
    row = np.repeat(u, side)
    col = np.tile(u, side)
    table = np.zeros((8, 128), np.float32)
    left = [np.concatenate([row, row]) / TURN, np.concatenate([col, col]) / TURN]
    for k in range(3):
        for n in range(2):
            part = left[n].astype(np.float32).astype(jnp.bfloat16).astype(np.float64)
            table[2 * k + n] = part
            left[n] = left[n] - part
    return table


def body(charges, leaf_slot, node_offset, lagrange, evaluate, parts=PARTS):
    vm = pl.BlockSpec(memory_space=pltpu.VMEM)
    comm = "comm" in parts
    cp = dict(collective_id=0) if comm else {}
    return pl.pallas_call(
        functools.partial(kernel, parts),
        out_shape=jax.ShapeDtypeStruct((64, 128, 128), BF16),
        in_specs=[vm, pl.BlockSpec(memory_space=pltpu.SMEM), vm, vm, vm, vm],
        out_specs=pl.BlockSpec(memory_space=pl.ANY),
        scratch_shapes=[
            pltpu.VMEM((256 * 33, 128), F32),
            pltpu.VMEM((4, 128, 16, 128), F32),
            pltpu.VMEM((4, 8, 128, 16, 256), BF16),
            pltpu.VMEM((128, 16, 128), BF16),
            pltpu.VMEM((4, 128, 16, 128), BF16),
            pltpu.VMEM((4, 128, 16, 128), BF16),
            pltpu.VMEM((64, 2, 128), F32),
            pltpu.VMEM((128, 2, 128), F32),
            pltpu.VMEM((128, 128), F32),
            pltpu.VMEM((512, 128), F32),
            pltpu.VMEM((512, 128), BF16),
            pltpu.VMEM((8, 128, 256), BF16),
            pltpu.VMEM((8192, 128), F32),
            pltpu.VMEM((256, 256), BF16),
            pltpu.VMEM((128, 128), BF16),
            pltpu.VMEM((4, 16, 128, 128), BF16),
            pltpu.VMEM((16 * 129, 128), F32),
            pltpu.SemaphoreType.DMA((4,)), pltpu.SemaphoreType.DMA((4,)),
            pltpu.SemaphoreType.DMA((1,)), pltpu.SemaphoreType.DMA((1,)), pltpu.SemaphoreType.DMA((4,)),
        ],
        compiler_params=pltpu.CompilerParams(has_side_effects=True, vmem_limit_bytes=60 << 20, **cp),
    )(charges, leaf_slot, node_offset, lagrange, evaluate, jnp.asarray(chebyshev_lanes()))


def solution(mesh, parts=PARTS):
    placed = (P(("gx", "gy"), None, None), P(("gx", "gy"), None), P(("gx", "gy"), None, None), P(), P())
    return jax.shard_map(functools.partial(body, parts=parts), mesh=mesh, in_specs=placed,
                         out_specs=P(("gx", "gy"), None, None), check_vma=False)
```

```python
import functools
import math

import jax
import jax.numpy as jnp
import numpy as np
from jax import lax
from jax.experimental import pallas as pl
from jax.experimental.pallas import tpu as pltpu
from jax.sharding import PartitionSpec as P

MESH = pl.DeviceIdType.MESH
F32 = jnp.float32
BF16 = jnp.bfloat16
TURN = 2.0 * math.pi
SIN_TERMS = None


def sine_terms():
    k = np.arange(400)
    w = 0.125 * (1 + np.cos(np.pi * (k + 0.5) / 400))
    v = w * w
    basis = np.stack([w * v**j for j in range(4)], axis=1)
    weight = 1.0 / np.sqrt(np.sin(TURN * w) + 1e-3)
    coef = np.linalg.lstsq(basis * weight[:, None], np.sin(TURN * w) * weight, rcond=None)[0]
    return [float(c) for c in coef]


SIN_TERMS = sine_terms()
TILES = 8
ROLL16 = True
PARTS = ("gather", "z1", "p1", "z2", "p2", "comm", "z3", "p3")


def cosine_turns(x):
    x = x - jnp.round(x)
    w = 0.25 - jnp.abs(x)
    v = w * w
    r = SIN_TERMS[3] * v + SIN_TERMS[2]
    r = r * v + SIN_TERMS[1]
    r = r * v + SIN_TERMS[0]
    return r * w


def swap(tile):
    if ROLL16:
        return pltpu.roll(tile, 64, 1)
    return pltpu.roll(tile.astype(F32), 64, 1).astype(BF16)


def kernel(parts, ch_ref, slot_ref, off_ref, lag_ref, ev_ref, nodes_ref, out_ref,
           cf, g, zt, x, send, recv, ab, ro, at, lh, lt, us, tau, w, ev, ob, o32, ssem, rsem, offs, offr, osem):
    gx, gy = lax.axis_index("gx"), lax.axis_index("gy")
    me = gx * 16 + gy
    comm = "comm" in parts
    if comm:
        bar = pltpu.get_barrier_semaphore()

        def greet(k):
            dst = (me + k) & 127
            pl.semaphore_signal(bar, inc=1, device_id=(dst >> 4, dst & 15), device_id_type=MESH)

        @pl.loop(1, 16)
        def _(k):
            greet(k)

    for e in range(2):
        for c in range(2):
            re = lag_ref[e, c, 0].astype(F32)
            im = lag_ref[e, c, 1].astype(F32)
            w[pl.ds(e * 128, 64), pl.ds(c * 128, 128)] = jnp.concatenate([re, im], axis=1).astype(BF16)
            w[pl.ds(e * 128 + 64, 64), pl.ds(c * 128, 128)] = jnp.concatenate([-im, re], axis=1).astype(BF16)
    re = ev_ref[0].astype(F32)
    im = ev_ref[1].astype(F32)
    ev[pl.ds(0, 64), :] = jnp.concatenate([re, im], axis=1).astype(BF16)
    ev[pl.ds(64, 64), :] = jnp.concatenate([-im, re], axis=1).astype(BF16)

    none = jnp.zeros((8, 128), F32)
    top = jnp.concatenate([nodes_ref[...], none], axis=1)
    bottom = jnp.concatenate([none, nodes_ref[...]], axis=1)
    us[...] = jnp.zeros((8, 128, 256), BF16)
    for p in range(8):
        us[p, pl.ds(16 * p, 16), :] = jnp.concatenate([top, bottom], axis=0).astype(BF16)

    for m in range(64):
        ab[m] = off_ref[0, :, pl.ds(m * 128, 128)].astype(F32)
    lane = lax.broadcasted_iota(jnp.int32, (16, 128), 1)
    low = lane < 64
    signed = jnp.where(low, 0.25, -0.25).astype(F32)
    wide = lax.broadcasted_iota(jnp.int32, (64, 128), 1) < 64

    def make_tau(oa, ob_):
        for k in range(3):
            lh[pl.ds(2 * k, 64, stride=8), :] = oa
            lh[pl.ds(2 * k + 1, 64, stride=8), :] = ob_
        for k in range(6, 8):
            lh[pl.ds(k, 64, stride=8), :] = jnp.zeros((64, 128), F32)
        for n in range(4):
            lt[pl.ds(n * 128, 128), :] = lh[pl.ds(n * 128, 128), :].T.astype(BF16)

        @pl.loop(0, 8, step=2)
        def _(p):
            for e in range(2):
                r = jnp.dot(lt[...], us[p + e], preferred_element_type=F32)
                for n in range(4):
                    row = pl.multiple_of((n * 16 + 2 * (p + e)) * 128, 128)
                    tau[pl.ds(row, 128), :] = r[n * 128:n * 128 + 128, 0:128]
                    tau[pl.ds(row + 128, 128), :] = r[n * 128:n * 128 + 128, 128:256]

    def start(t, first):
        c1 = cosine_turns(t)
        s1 = cosine_turns(t + signed)
        twice = 2.0 * c1
        if first == 1:
            return (c1, s1), (1.0, 0.0), twice
        c2, s2 = twice * c1 - 1.0, twice * s1
        if first == 8:
            k2 = 2.0 * c2
            c4, s4 = k2 * c2 - 1.0, k2 * s2
            k4 = 2.0 * c4
            c8, s8 = k4 * c4 - 1.0, k4 * s4
            return (c8, s8), (c8 * c1 + s8 * s1, s8 * c1 - c8 * s1), twice
        c3, s3 = twice * c2 - c1, twice * s2 - s1
        k3 = 2.0 * c3
        c6, s6 = k3 * c3 - 1.0, k3 * s3
        c7, s7 = c6 * c1 - s6 * s1, s6 * c1 + c6 * s1
        k7 = 2.0 * c7
        c14, s14 = k7 * c7 - 1.0, k7 * s7
        return (c14, s14), (c14 * c1 + s14 * s1, s14 * c1 - c14 * s1), twice

    def phase_tiles(i, slot, first, count, j, tiles):
        state = [start(tau[pl.ds((j + n) * 64 + i * 16, 16), :], first) for n in range(tiles)]
        for l in range(count):
            for n in range(tiles):
                now, before, twice = state[n]
                zt[slot, l, j + n, :, pl.ds(0, 128)] = now[0].astype(BF16)
                zt[slot, l, j + n, :, pl.ds(128, 128)] = now[1].astype(BF16)
                if l + 1 < count:
                    state[n] = ((twice * now[0] - before[0], twice * now[1] - before[1]), now, twice)

    def many_phases(i, slot, first, count):
        @pl.loop(0, 128, step=TILES)
        def _(j):
            phase_tiles(i, slot, first, count, j, TILES)

    def turned(tile, i, l, q):
        return tile * zt[i, l, q, :, pl.ds(0, 128)] + swap(tile) * zt[i, l, q, :, pl.ds(128, 128)]

    def level(i, l, bit, load, save, per=32):
        for blk in range(64 // per):
            rows = []
            idx = []
            for p in range(blk * per, (blk + 1) * per):
                q0 = ((p >> bit) << (bit + 1)) | (p & ((1 << bit) - 1))
                q1 = q0 | (1 << bit)
                idx.append((q0, q1))
                rows.append(jnp.concatenate([turned(load(q0), i, l, q0), turned(load(q1), i, l, q1)], axis=1))
            o = jnp.dot(jnp.concatenate(rows, axis=0), w[...], preferred_element_type=F32)
            for j, (q0, q1) in enumerate(idx):
                save(q0, o[16 * j:16 * j + 16, 0:128])
                save(q1, o[16 * j:16 * j + 16, 128:256])

    def load_x(q):
        return x[q]

    def save_x(q, v):
        x[q] = v.astype(BF16)

    pair = []
    for k in range(2):
        rows = ab[:, k, :]
        at[...] = jnp.concatenate([rows, rows], axis=0).T
        pair.append(jnp.where(wide, at[pl.ds(0, 64, stride=2), :], at[pl.ds(1, 64, stride=2), :]))
    make_tau(*pair)

    @pl.loop(0, 8)
    def _(j):
        cf[pl.ds(j * 1024, 1024), :] = ch_ref[0, pl.ds(j * 1024, 1024), :].astype(F32)

    @pl.loop(0, 4)
    def _(i):
        @pl.loop(0, 128, step=TILES)
        def _(j):
            if comm:
                greet(16 + i * 16 + j // 8)
            if "z1" in parts:
                phase_tiles(i, i, 1, 7, j, TILES)
            if "gather" in parts:
                for n in range(TILES):
                    for r in range(16):
                        slot = slot_ref[0, (i * 16 + r) * 128 + j + n]
                        g[i, j + n, pl.ds(r, 1), :] = cf[pl.ds(slot, 1), :]

    if "p1" in parts:
        @pl.loop(0, 4)
        def _(i):
            for n in range(12 if comm else 0):
                greet(80 + i * 12 + n)
            for l in range(7):
                load = load_x if l > 0 else (lambda q: g[i, q].astype(BF16))
                if l < 6:
                    save = save_x
                else:
                    def save(q, v):
                        c, t, hi = (q >> 4) & 3, q & 15, q >> 6
                        cf[pl.ds((c * 64 + 16 * i) * 33 + hi * 16 + t, 16, stride=33), :] = v
                level(i, l, l, load, save)

    if comm:
        pl.semaphore_wait(bar, 127)

        @pl.loop(1, 128)
        def _(k):
            dst = (me + k) & 127
            pltpu.make_async_remote_copy(src_ref=ab.at[dst >> 1], dst_ref=ro.at[me], send_sem=offs.at[0],
                                         recv_sem=offr.at[0], device_id=(dst >> 4, dst & 15), device_id_type=MESH).start()
        pltpu.make_async_copy(ab.at[me >> 1], ro.at[me], offr.at[0]).start()

    make_tau(ab[:, 0, :], ab[:, 1, :])

    @pl.loop(0, 4)
    def _(c):
        if "z2" in parts:
            many_phases(c, 0, 8, 6)
        if "p2" in parts:
            for l in range(6):
                load = load_x if l > 0 else (lambda q: cf[pl.ds((c * 64 + (q >> 1)) * 33 + (q & 1) * 16, 16), :].astype(BF16))
                if l < 5:
                    save = save_x
                else:
                    def save(q, v):
                        send[c, q] = v.astype(BF16)
                level(0, l, l + 1, load, save)
        if comm:
            @pl.loop(1, 128)
            def _(k):
                dst = (me + k) & 127
                pltpu.make_async_remote_copy(src_ref=send.at[c, dst], dst_ref=recv.at[c, me], send_sem=ssem.at[c],
                                             recv_sem=rsem.at[c], device_id=(dst >> 4, dst & 15), device_id_type=MESH).start()
            pltpu.make_async_copy(send.at[c, me], recv.at[c, me], rsem.at[c]).start()

    if comm:
        pltpu.make_async_copy(ro, ro, offr.at[0]).wait()
    odd = jnp.full((64, 128), me & 1, jnp.int32) == 1
    pair = []
    for k in range(2):
        first, second = ro[pl.ds(0, 64, stride=2), k, :], ro[pl.ds(1, 64, stride=2), k, :]
        even_half = jnp.where(wide, first, pltpu.roll(second, 64, 1))
        odd_half = jnp.where(wide, pltpu.roll(first, 64, 1), second)
        pair.append(jnp.where(odd, odd_half, even_half))
    make_tau(*pair)

    if "z3" in parts:
        @pl.loop(0, 4)
        def _(c):
            many_phases(c, c, 14, 8)

    @pl.loop(0, 4)
    def _(c):
        if comm:
            pltpu.make_async_copy(recv.at[c], recv.at[c], rsem.at[c]).wait()
        if "p3" in parts:
            for l in range(7):
                level(c, l, l, load_x if l > 0 else (lambda q: recv[c, q]), save_x)
            for blk in range(4):
                rows = jnp.concatenate([turned(x[q], c, 7, q) for q in range(blk * 32, blk * 32 + 32)], axis=0)
                v = jnp.dot(rows, ev[...], preferred_element_type=F32)
                for j in range(32):
                    o32[pl.ds(blk * 32 + j, 16, stride=129), :] = v[16 * j:16 * j + 16]
            for t in range(16):
                ob[c, t] = o32[pl.ds(t * 129, 128), :].astype(BF16)
        pltpu.make_async_copy(ob.at[c], out_ref.at[pl.ds(c * 16, 16)], osem.at[c]).start()

    for c in range(4):
        pltpu.make_async_copy(ob.at[c], out_ref.at[pl.ds(c * 16, 16)], osem.at[c]).wait()
    if comm:
        pltpu.make_async_copy(ro.at[pl.ds(0, 127)], ro.at[pl.ds(0, 127)], offs.at[0]).wait()
        for c in range(4):
            pltpu.make_async_copy(recv.at[c, pl.ds(0, 127)], recv.at[c, pl.ds(0, 127)], ssem.at[c]).wait()


def chebyshev_lanes():
    side = 8
    u = np.cos(math.pi * (2.0 * np.arange(side) + 1.0) / (2.0 * side))
    row = np.repeat(u, side)
    col = np.tile(u, side)
    table = np.zeros((8, 128), np.float32)
    left = [np.concatenate([row, row]) / TURN, np.concatenate([col, col]) / TURN]
    for k in range(3):
        for n in range(2):
            part = left[n].astype(np.float32).astype(jnp.bfloat16).astype(np.float64)
            table[2 * k + n] = part
            left[n] = left[n] - part
    return table


def body(charges, leaf_slot, node_offset, lagrange, evaluate, parts=PARTS):
    vm = pl.BlockSpec(memory_space=pltpu.VMEM)
    comm = "comm" in parts
    cp = dict(collective_id=0) if comm else {}
    return pl.pallas_call(
        functools.partial(kernel, parts),
        out_shape=jax.ShapeDtypeStruct((64, 128, 128), BF16),
        in_specs=[vm, pl.BlockSpec(memory_space=pltpu.SMEM), vm, vm, vm, vm],
        out_specs=pl.BlockSpec(memory_space=pl.ANY),
        scratch_shapes=[
            pltpu.VMEM((256 * 33, 128), F32),
            pltpu.VMEM((4, 128, 16, 128), F32),
            pltpu.VMEM((4, 8, 128, 16, 256), BF16),
            pltpu.VMEM((128, 16, 128), BF16),
            pltpu.VMEM((4, 128, 16, 128), BF16),
            pltpu.VMEM((4, 128, 16, 128), BF16),
            pltpu.VMEM((64, 2, 128), F32),
            pltpu.VMEM((128, 2, 128), F32),
            pltpu.VMEM((128, 128), F32),
            pltpu.VMEM((512, 128), F32),
            pltpu.VMEM((512, 128), BF16),
            pltpu.VMEM((8, 128, 256), BF16),
            pltpu.VMEM((8192, 128), F32),
            pltpu.VMEM((256, 256), BF16),
            pltpu.VMEM((128, 128), BF16),
            pltpu.VMEM((4, 16, 128, 128), BF16),
            pltpu.VMEM((16 * 129, 128), F32),
            pltpu.SemaphoreType.DMA((4,)), pltpu.SemaphoreType.DMA((4,)),
            pltpu.SemaphoreType.DMA((1,)), pltpu.SemaphoreType.DMA((1,)), pltpu.SemaphoreType.DMA((4,)),
        ],
        compiler_params=pltpu.CompilerParams(has_side_effects=True, vmem_limit_bytes=60 << 20, **cp),
    )(charges, leaf_slot, node_offset, lagrange, evaluate, jnp.asarray(chebyshev_lanes()))


def solution(mesh, parts=PARTS):
    placed = (P(("gx", "gy"), None, None), P(("gx", "gy"), None), P(("gx", "gy"), None, None), P(), P())
    return jax.shard_map(functools.partial(body, parts=parts), mesh=mesh, in_specs=placed,
                         out_specs=P(("gx", "gy"), None, None), check_vma=False)
```
